32 devices in a mesh: section: 4 (over z), ctx: 8 (over y, x, core).
Axes of the slice: x: 2, y: 2, z: 4, core: 2. Of those that a mesh axis runs over, the one named last changes fastest.
Arguments:
- spins: int32 [4, 1024], replicated, may hold values from 0 to 1
- block_mask: int32 [8, 8], P('ctx'), may hold values from 0 to 1, as said below
- tok_embed: float32 [3, 1024], replicated, may hold values from -6 to 6
- pos_embed: bfloat16 [1024, 1024], P('ctx'), may hold values from -6 to 6
- norm1_gain: float32 [4, 1024], P('section'), may hold values from 0.1 to 1.9
- w_qkv: bfloat16 [4, 1024, 3072], P('section')
- w_out: bfloat16 [4, 1024, 1024], P('section'), may hold values from -0.1875 to 0.1875
- norm2_gain: float32 [4, 1024], P('section'), may hold values from 0.1 to 1.9
- w_up: bfloat16 [4, 1024, 2048], P('section'), may hold values from -0.1875 to 0.1875
- w_down: bfloat16 [4, 2048, 1024], P('section'), may hold values from -0.125 to 0.125
- w_head: float32 [1024], replicated, may hold values from -0.1875 to 0.1875
Outputs:
- log_amplitude: float32 [4, 1024], P('section', 'ctx')
The draws below stay inside these ranges and needn't reach their ends.
Inputs may be any that keep to these rules, and one draw needn't show every extreme that they name: block_mask[q, k] is 1 where k = q, and where k = q - 1; where q - k = 2 ** j with 1 <= j < 3 it is 0 or 1; it is 0 everywhere else.
All inputs are finite; a program needn't handle non-finite values.
Results may differ from the reference program's by a relative error of at most 0.012.
Values may be sent and summed in bfloat16 or wider, within the bound.
A program may use at most 64 MiB of HBM per device.

```python
import math
import jax
import jax.numpy as jnp
from jax import lax

D = 1024
HEADS = 16
FF = 2048
BLOCK = 128
NDIL = 3
LAYERS = 4
SAMPLES = 4
L = 1024
NBLK = 8


def draw_block_mask(key, part):
    query_index = jnp.arange(NBLK, dtype=jnp.int32)[:, None]
    key_index = jnp.arange(NBLK, dtype=jnp.int32)[None, :]
    distance = query_index - key_index
    coins = jax.random.randint(key, (NBLK, NBLK), 0, 2)
    dilated = jnp.zeros((NBLK, NBLK), jnp.bool_)
    for level_index in range(1, NDIL):
        dilated = dilated | (distance == 2 ** level_index)
    local = (distance == 0) | (distance == 1)
    return jnp.where(local, 1, jnp.where(dilated, coins, 0)).astype(jnp.int32)


def draw_w_qkv(key, part):
    base = jnp.clip(jax.random.normal(key, (LAYERS, D, 3 * D), jnp.float32), -6.0, 6.0) * D ** (-0.5)
    return base.astype(jnp.bfloat16)


def touch_ends(result, stream_key, least, high):
    dims = result.shape
    index_at = [jax.random.randint(jax.random.fold_in(stream_key, axis), (), 0, dims[axis]) for axis in range(len(dims))]
    result = result.at[tuple(index_at)].set(least)
    longest = dims.index(max(dims))
    index_at[longest] = (index_at[longest] + 1) % dims[longest]
    return result.at[tuple(index_at)].set(high)


def steps_of(stream_key, dims, pieces, least, high):
    loudness = 1.0
    for position, parts in pieces:
        heights = jax.random.uniform(jax.random.fold_in(jax.random.fold_in(stream_key, 6), position), (parts,), jnp.float32, least / len(pieces), high / len(pieces))
        loudness = loudness * jnp.repeat(jnp.exp(heights), dims[position] // parts).reshape((-1,) + (1,) * (len(dims) - 1 - position))
    return loudness


def noise(rng, shape, spread, most, shards=(), kind=jnp.bfloat16):
    result = jax.random.normal(rng, shape, jnp.float32) * spread
    if len(shards) > 0:
        result = steps_of(rng, shape, shards, -0.22, 0.18) * result
    return jnp.clip(result, min=-most, max=most).astype(kind)


def setup_inputs(seed: int = 0) -> dict:
    arg_keys = jax.random.split(jax.random.key(seed), 12)
    spins = touch_ends(jax.random.randint(arg_keys[0], (SAMPLES, L), 0, 2), jax.random.fold_in(arg_keys[0], 1), 0, 1).astype(jnp.int32)
    block_mask = draw_block_mask(jax.random.fold_in(arg_keys[11], 71), 0)
    tok_embed = noise(arg_keys[2], (3, D), 1.0, 6.0, (), jnp.float32)
    pos_embed = noise(arg_keys[3], (L, D), 1.0, 6.0, ((0, 8),))
    norm1_gain = jnp.clip(1.0 + 0.18 * jax.random.normal(arg_keys[4], (LAYERS, D), jnp.float32), 0.1, 1.9)
    w_qkv = draw_w_qkv(jax.random.fold_in(arg_keys[11], 71), 0)
    w_out = noise(arg_keys[6], (LAYERS, D, D), D ** -0.5, 0.1875, ((0, 4),))
    norm2_gain = jnp.clip(1.0 + 0.18 * jax.random.normal(arg_keys[7], (LAYERS, D), jnp.float32), 0.1, 1.9)
    w_up = noise(arg_keys[8], (LAYERS, D, FF), D ** -0.5, 0.1875, ((0, 4),))
    w_down = noise(arg_keys[9], (LAYERS, FF, D), FF ** -0.5, 0.125, ((0, 4),))
    w_head = noise(arg_keys[10], (D,), D ** -0.5, 0.1875, (), jnp.float32)
    return dict(spins=spins, block_mask=block_mask, tok_embed=tok_embed, pos_embed=pos_embed, norm1_gain=norm1_gain, w_qkv=w_qkv, w_out=w_out, norm2_gain=norm2_gain, w_up=w_up, w_down=w_down, w_head=w_head)


def rms_normed(vector):
    return vector * lax.rsqrt(lax.optimization_barrier(jnp.mean(vector * vector, axis=-1, keepdims=True)) + 1e-05)

def attend(queries, key_rows, value_rows, block_mask):
    samples, length, head_count, head_dim = queries.shape
    block_count = length // BLOCK
    window = 2 ** (NDIL - 1) + 1
    padding = (window - 1) * BLOCK
    keys_padded = jnp.pad(key_rows, ((0, 0), (padding, 0), (0, 0), (0, 0)))
    values_padded = jnp.pad(value_rows, ((0, 0), (padding, 0), (0, 0), (0, 0)))
    key_slot = jnp.arange(window * BLOCK, dtype=jnp.int32)
    query_pos = jnp.arange(BLOCK, dtype=jnp.int32)

    def one_block(block_index):
        query_block = lax.dynamic_slice_in_dim(queries, block_index * BLOCK, BLOCK, 1).astype(jnp.float32)
        key_block = lax.dynamic_slice_in_dim(keys_padded, block_index * BLOCK, window * BLOCK, 1).astype(jnp.float32)
        value_block = lax.dynamic_slice_in_dim(values_padded, block_index * BLOCK, window * BLOCK, 1).astype(jnp.float32)
        scores = jnp.einsum('sqhd,skhd->shqk', query_block, key_block) / math.sqrt(head_dim)
        key_block_index = block_index - (window - 1) + key_slot // BLOCK
        key_pos = key_slot % BLOCK
        mask_row = lax.dynamic_index_in_dim(block_mask, block_index, 0, keepdims=False)
        picked = mask_row[jnp.clip(key_block_index, 0, block_count - 1)]
        earlier = (key_block_index >= 0) & (key_block_index < block_index) & (picked == 1)
        same_block = (key_block_index == block_index)[None, :] & (key_pos[None, :] <= query_pos[:, None])
        allowed = same_block | earlier[None, :]
        scores = jnp.where(allowed[None, None], scores, -jnp.inf)
        probs = jax.nn.softmax(scores, axis=-1).astype(jnp.bfloat16)
        mixed = jnp.einsum('shqk,skhd->sqhd', probs.astype(jnp.float32), value_block)
        return mixed.astype(jnp.bfloat16)
    blocks = lax.map(one_block, jnp.arange(block_count, dtype=jnp.int32))
    return jnp.transpose(blocks, (1, 0, 2, 3, 4)).reshape(samples, length, head_count * head_dim)

def reference(spins, block_mask, tok_embed, pos_embed, norm1_gain, w_qkv, w_out, norm2_gain, w_up, w_down, w_head):
    samples, length = spins.shape
    head_dim = D // HEADS
    previous = jnp.concatenate([jnp.full((samples, 1), 2, jnp.int32), spins[:, :-1]], axis=1)[..., None]
    embedded = jnp.where(previous == 0, tok_embed[0], jnp.where(previous == 1, tok_embed[1], tok_embed[2]))
    state = (embedded + pos_embed.astype(jnp.float32)[None]).astype(jnp.bfloat16)
    for layer_index in range(LAYERS):
        normed_rows = (rms_normed(state.astype(jnp.float32)) * norm1_gain[layer_index]).astype(jnp.bfloat16)
        projected = jnp.dot(normed_rows.reshape(-1, D), w_qkv[layer_index], preferred_element_type=jnp.float32)
        queries = projected[:, :D].astype(jnp.bfloat16).reshape(samples, length, HEADS, head_dim)
        key_rows = projected[:, D:2 * D].astype(jnp.bfloat16).reshape(samples, length, HEADS, head_dim)
        value_rows = projected[:, 2 * D:].astype(jnp.bfloat16).reshape(samples, length, HEADS, head_dim)
        attended = attend(queries, key_rows, value_rows, block_mask)
        hidden = state.astype(jnp.float32) + jnp.dot(attended.reshape(-1, D), w_out[layer_index], preferred_element_type=jnp.float32).reshape(samples, length, D)
        lifted = (rms_normed(hidden) * norm2_gain[layer_index]).astype(jnp.bfloat16)
        activated = jax.nn.gelu(jnp.dot(lifted.reshape(-1, D), w_up[layer_index], preferred_element_type=jnp.float32)).astype(jnp.bfloat16)
        state = (hidden + jnp.dot(activated, w_down[layer_index], preferred_element_type=jnp.float32).reshape(samples, length, D)).astype(jnp.bfloat16)
    final_rows = rms_normed(state.astype(jnp.float32))
    logits = jnp.dot(final_rows.reshape(-1, D), w_head, precision=lax.Precision.HIGHEST).reshape(samples, length)
    per_site_terms = math.log(2.0) - jax.nn.softplus((1.0 - 2.0 * spins.astype(jnp.float32)) * logits)
    return 0.5 * jnp.cumsum(per_site_terms, axis=1)
```

```python
import functools
import math

import jax
import jax.numpy as jnp
from jax import lax
from jax.experimental import pallas as pl
from jax.experimental.pallas import tpu as pltpu
from jax.sharding import PartitionSpec as P

HEADS = 16
NDIL = 3
CORES = 2
LANES = 128
PARTS = 2
MASKED = -1e30


def rms_normed(vector):
    return vector * lax.rsqrt(jnp.mean(vector * vector, axis=-1, keepdims=True) + 1e-05)


def kernel(
    sections,
    ctx_count,
    spins_ref,
    mask_ref,
    tok_ref,
    pos_hbm,
    gain1_ref,
    wqkv_hbm,
    wout_hbm,
    gain2_ref,
    wup_hbm,
    wdown_hbm,
    whead_ref,
    out_ref,
    wqkv,
    wout,
    wup,
    wdown,
    pos,
    xin,
    xout,
    kv_own,
    kv_far,
    queries,
    attended,
    activated,
    hidden,
    bias,
    mask_send,
    mask_rows,
    totals_send,
    totals_far,
    rows_keep,
    result_send,
    result_in,
    w_sem,
    pos_local_sem,
    pos_send_sem,
    pos_recv_sem,
    mask_send_sem,
    mask_recv_sem,
    x_send_sem,
    x_recv_sem,
    kv_send_sem,
    kv_recv_sem,
    tot_send_sem,
    tot_recv_sem,
    res_send_sem,
    res_recv_sem,
):
    ticks = ctx_count // CORES
    groups = ticks
    block_len, width = pos.shape[1], pos.shape[2]
    part_width = width // PARTS
    hid = wup.shape[1]
    head_dim = width // HEADS
    s = lax.axis_index("section")
    b = lax.axis_index("ctx")
    n = b // CORES
    c = b % CORES
    partner = b + 1 - 2 * c
    last = sections - 1

    def ring(step):
        return lax.rem(n + step, groups)

    w_copies = [
        pltpu.make_async_copy(wqkv_hbm.at[0], wqkv, w_sem.at[0]),
        pltpu.make_async_copy(wout_hbm.at[0], wout, w_sem.at[1]),
        pltpu.make_async_copy(wup_hbm.at[0], wup, w_sem.at[2]),
        pltpu.make_async_copy(wdown_hbm.at[0], wdown, w_sem.at[3]),
    ]
    pos_local = pltpu.make_async_copy(pos_hbm, pos.at[n], pos_local_sem)

    @pl.when(s == 0)
    def _():
        pos_local.start()

    for copy in w_copies:
        copy.start()

    barrier = pltpu.get_barrier_semaphore()

    def greet(section, ctx):
        pl.semaphore_signal(
            barrier, inc=1, device_id=(section, ctx), device_id_type=pl.DeviceIdType.MESH
        )

    greet(s, partner)
    for step in range(1, groups):
        greet(s, ring(step) * CORES + c)

    @pl.when(s > 0)
    def _():
        greet(s - 1, b)

    result_from = s * CORES + c
    from_self = (s == last) & (b == result_from)

    @pl.when(jnp.logical_not(from_self))
    def _():
        greet(last, result_from)

    lane = lax.broadcasted_iota(jnp.int32, (8, LANES), 1)
    mask_send[...] = jnp.zeros((8, LANES), jnp.float32)
    mask_send[0:1, 0:ctx_count] = mask_ref[...].astype(jnp.float32)
    mask_rows[n] = mask_send[...]

    blank = jnp.zeros((block_len, 2 * width), jnp.bfloat16)
    for slot in range(1 << (NDIL - 2)):
        kv_own[slot] = blank
    kv_far[0] = blank

    receivers = groups + jnp.where(
        s < last, 1, ticks - jnp.where(n == last, 1, 0)
    )
    pl.semaphore_wait(barrier, receivers)

    def remote(src, dst, send_sem, recv_sem, section, ctx):
        return pltpu.make_async_remote_copy(
            src_ref=src,
            dst_ref=dst,
            send_sem=send_sem,
            recv_sem=recv_sem,
            device_id=(section, ctx),
            device_id_type=pl.DeviceIdType.MESH,
        )

    def mask_copy(step):
        return remote(
            mask_send, mask_rows.at[n], mask_send_sem.at[step], mask_recv_sem.at[n],
            s, ring(step) * CORES + c,
        )

    def pos_copy(step):
        return remote(
            pos_hbm, pos.at[n], pos_send_sem.at[step], pos_recv_sem.at[n],
            0, ring(step) * CORES + c,
        )

    for step in range(1, groups):
        mask_copy(step).start()

    @pl.when(s == 0)
    def _():
        for step in range(1, groups):
            pos_copy(step).start()

    def mask_arrival(slot):
        return remote(
            mask_send, mask_rows.at[slot], mask_send_sem.at[0], mask_recv_sem.at[slot], s, partner
        )

    def pos_arrival(slot):
        return remote(pos_hbm, pos.at[slot], pos_send_sem.at[0], pos_recv_sem.at[slot], 0, partner)

    def x_copy(j, part):
        return remote(
            xout.at[j, part], xin.at[j, part], x_send_sem.at[j, part], x_recv_sem.at[j, part],
            s + 1, b,
        )

    def kv_copy(j):
        return remote(
            kv_own.at[j + (1 << (NDIL - 2))], kv_far.at[j + 1], kv_send_sem.at[j],
            kv_recv_sem.at[j + 1], s, partner,
        )

    def kv_arrival(slot):
        return remote(
            kv_far.at[slot], kv_far.at[slot], kv_send_sem.at[0], kv_recv_sem.at[slot], s, partner
        )

    def total_copy(j):
        return remote(
            totals_send.at[j], totals_far.at[j], tot_send_sem.at[j], tot_recv_sem.at[j], s, partner
        )

    row_at = lax.broadcasted_iota(jnp.int32, (block_len, block_len), 0)
    col_at = lax.broadcasted_iota(jnp.int32, (block_len, block_len), 1)

    def spins_row(block):
        at = pl.multiple_of(block * block_len, block_len)
        rows = spins_ref[:, pl.ds(at, block_len)].astype(jnp.float32)
        which = lax.broadcasted_iota(jnp.int32, rows.shape, 0)
        return jnp.sum(jnp.where(which == n, rows, 0.0), axis=0, keepdims=True)

    def tick(j, carry):
        block = j * CORES + c

        @pl.when(j != n)
        def _():
            mask_arrival(j).wait_recv()

        flags = mask_rows[j]
        bias[:, 0:block_len] = jnp.where(col_at <= row_at, 0.0, MASKED)
        for level in range(NDIL):
            source = block - (1 << level)
            hit = jnp.where((lane == source) & (flags > 0.5), 1.0, 0.0)
            hit = jnp.sum(hit[0:1], axis=1, keepdims=True)
            bias[:, (level + 1) * block_len : (level + 2) * block_len] = jnp.broadcast_to(
                jnp.where(hit > 0.5, 0.0, MASKED), (block_len, block_len)
            )

        @pl.when(s == 0)
        def _():
            @pl.when(j == n)
            def _():
                pos_local.wait()

            @pl.when(j != n)
            def _():
                pos_arrival(j).wait_recv()

            row = spins_row(block)
            before = spins_row(jnp.maximum(block - 1, 0))[:, block_len - 1 : block_len]
            first = jnp.where(block > 0, before, 2.0)
            token = jnp.sum(jnp.where(col_at == row_at - 1, row, 0.0), axis=1, keepdims=True)
            token = jnp.where(row_at[:, 0:1] == 0, first, token)
            rows = jnp.where(
                token == 0.0,
                tok_ref[0:1, :],
                jnp.where(token == 1.0, tok_ref[1:2, :], tok_ref[2:3, :]),
            )
            rows = (rows + pos[j].astype(jnp.float32)).astype(jnp.bfloat16)
            for part in range(PARTS):
                xin[j, part] = rows[:, part * part_width : (part + 1) * part_width]

        @pl.when(s > 0)
        def _():
            for part in range(PARTS):
                remote(
                    xout.at[j, part], xin.at[j, part], x_send_sem.at[j, part],
                    x_recv_sem.at[j, part], s, partner,
                ).wait_recv()

        layer_in = jnp.concatenate([xin[j, part] for part in range(PARTS)], axis=1)
        layer_in = layer_in.astype(jnp.float32)
        hidden[...] = layer_in
        normed = (rms_normed(layer_in) * gain1_ref[...]).astype(jnp.bfloat16)

        @pl.when(j == 0)
        def _():
            w_copies[0].wait()

        own = j + (1 << (NDIL - 2))
        for chunk in range(width, 3 * width, 512):
            kv_own[own, :, chunk - width : chunk - width + 512] = jnp.dot(
                normed, wqkv[:, chunk : chunk + 512], preferred_element_type=jnp.float32
            ).astype(jnp.bfloat16)

        @pl.when((c == 0) | (j < ticks - 1))
        def _():
            kv_copy(j).start()

        for chunk in range(0, width, 512):
            queries[:, chunk : chunk + 512] = (
                jnp.dot(normed, wqkv[:, chunk : chunk + 512], preferred_element_type=jnp.float32)
                .astype(jnp.bfloat16)
                .astype(jnp.float32)
                * (1.0 / math.sqrt(head_dim))
            ).astype(jnp.bfloat16)

        @pl.when(j + c > 0)
        def _():
            kv_arrival(j + c).wait_recv()

        key_slots = [(kv_own, own), (kv_far, j + c)]
        for level in range(1, NDIL):
            key_slots.append((kv_own, own - (1 << (level - 1))))
        bias_two = jnp.concatenate([bias[...], bias[...]], axis=0)
        lane_low = lax.broadcasted_iota(jnp.int32, (block_len, LANES), 1) < head_dim
        for pair in range(width // LANES):
            cols = slice(pair * LANES, (pair + 1) * LANES)
            vcols = slice(width + pair * LANES, width + (pair + 1) * LANES)
            q_pair = queries[:, cols]
            zero = jnp.zeros_like(q_pair)
            q_two = jnp.concatenate(
                [jnp.where(lane_low, q_pair, zero), jnp.where(lane_low, zero, q_pair)], axis=0
            )
            keys = jnp.concatenate([ref[at, :, cols] for ref, at in key_slots], axis=0)
            values = jnp.concatenate([ref[at, :, vcols] for ref, at in key_slots], axis=0)
            scores = lax.dot_general(
                q_two, keys, (((1,), (1,)), ((), ())), preferred_element_type=jnp.float32
            )
            scores = scores + bias_two
            top = jnp.max(scores, axis=1, keepdims=True)
            probs = jnp.exp(scores - top)
            norm = jnp.sum(probs, axis=1, keepdims=True)
            mixed = jnp.dot(
                probs.astype(jnp.bfloat16), values, preferred_element_type=jnp.float32
            ) / norm
            attended[:, cols] = jnp.where(
                lane_low, mixed[:block_len], mixed[block_len:]
            ).astype(jnp.bfloat16)

        @pl.when(j == 0)
        def _():
            w_copies[1].wait()

        att = attended[...]
        for chunk in range(0, width, 512):
            hidden[:, chunk : chunk + 512] += jnp.dot(
                att, wout[:, chunk : chunk + 512], preferred_element_type=jnp.float32
            )
        lifted = (rms_normed(hidden[...]) * gain2_ref[...]).astype(jnp.bfloat16)

        @pl.when(j == 0)
        def _():
            w_copies[2].wait()

        for chunk in range(0, hid, 512):
            activated[:, chunk : chunk + 512] = jax.nn.gelu(
                jnp.dot(lifted, wup[:, chunk : chunk + 512], preferred_element_type=jnp.float32)
            ).astype(jnp.bfloat16)

        @pl.when(j == 0)
        def _():
            w_copies[3].wait()

        act = activated[...]
        for part in range(PARTS):
            cols = slice(part * part_width, (part + 1) * part_width)
            xout[j, part] = (
                hidden[:, cols]
                + jnp.dot(act, wdown[:, cols], preferred_element_type=jnp.float32)
            ).astype(jnp.bfloat16)

            @pl.when(s < last)
            def _():
                x_copy(j, part).start()

        @pl.when(s == last)
        def _():
            final = jnp.concatenate([xout[j, part] for part in range(PARTS)], axis=1)
            final = rms_normed(final.astype(jnp.float32))
            logits = jnp.sum(final * whead_ref[...], axis=1, keepdims=True)
            spin_col = jnp.sum(
                jnp.where(col_at == row_at, spins_row(block), 0.0), axis=1, keepdims=True
            )
            signed = (1.0 - 2.0 * spin_col) * logits
            soft = jnp.maximum(signed, 0.0) + jnp.log1p(jnp.exp(-jnp.abs(signed)))
            terms = math.log(2.0) - soft
            running = jnp.sum(jnp.where(row_at <= col_at, terms, 0.0), axis=0, keepdims=True)
            total = jnp.sum(terms, axis=0, keepdims=True)
            rows_keep[j] = jnp.broadcast_to(running, (8, LANES))
            totals_send[j] = jnp.broadcast_to(total, (8, LANES))
            total_copy(j).start()

        return carry

    lax.fori_loop(0, ticks, tick, 0)

    def result_copy(j, section, ctx):
        return remote(
            result_send.at[j], result_in, res_send_sem.at[j], res_recv_sem, section, ctx
        )

    @pl.when(s == last)
    def _():
        offset = jnp.zeros((8, LANES), jnp.float32)
        for j in range(ticks):
            total_copy(j).wait_recv()
            own_total = totals_send[j]
            far_total = totals_far[j]
            before = offset + far_total * c.astype(jnp.float32)
            result = 0.5 * (rows_keep[j] + before)
            result_send[j] = result
            offset = offset + (own_total + far_total)
            to_self = (n == last) & (j == last)

            @pl.when(to_self)
            def _():
                result_in[...] = result

            @pl.when(jnp.logical_not(to_self))
            def _():
                result_copy(j, n, j * CORES + c).start()

    @pl.when(jnp.logical_not(from_self))
    def _():
        result_copy(0, s, partner).wait_recv()

    out_ref[...] = result_in[0:1, :]

    for step in range(1, groups):
        mask_copy(step).wait_send()

    @pl.when(s == 0)
    def _():
        for step in range(1, groups):
            pos_copy(step).wait_send()

    for j in range(ticks):
        @pl.when((c == 0) | (j < ticks - 1))
        def _():
            kv_copy(j).wait_send()

        @pl.when(s < last)
        def _():
            for part in range(PARTS):
                x_copy(j, part).wait_send()

        @pl.when(s == last)
        def _():
            total_copy(j).wait_send()

            @pl.when(jnp.logical_not((n == last) & (j == last)))
            def _():
                result_copy(j, n, j * CORES + c).wait_send()


def body(
    spins,
    block_mask,
    tok_embed,
    pos_embed,
    norm1_gain,
    w_qkv,
    w_out,
    norm2_gain,
    w_up,
    w_down,
    w_head,
):
    sections = lax.axis_size("section")
    ctx_count = lax.axis_size("ctx")
    ticks = ctx_count // CORES
    block_len, width = pos_embed.shape
    hid = w_up.shape[2]
    assert ticks == sections == spins.shape[0] and block_len == LANES
    bf16, f32 = jnp.bfloat16, jnp.float32
    vmem = pl.BlockSpec(memory_space=pltpu.VMEM)
    hbm = pl.BlockSpec(memory_space=pltpu.HBM)
    back = 1 << (NDIL - 2)
    dma = pltpu.SemaphoreType.DMA
    return pl.pallas_call(
        functools.partial(kernel, sections, ctx_count),
        out_shape=jax.ShapeDtypeStruct((1, block_len), f32),
        in_specs=[vmem, vmem, vmem, hbm, vmem, hbm, hbm, vmem, hbm, hbm, vmem],
        out_specs=vmem,
        scratch_shapes=[
            pltpu.VMEM((width, 3 * width), bf16),
            pltpu.VMEM((width, width), bf16),
            pltpu.VMEM((width, hid), bf16),
            pltpu.VMEM((hid, width), bf16),
            pltpu.VMEM((ticks, block_len, width), bf16),
            pltpu.VMEM((ticks, PARTS, block_len, width // PARTS), bf16),
            pltpu.VMEM((ticks, PARTS, block_len, width // PARTS), bf16),
            pltpu.VMEM((ticks + back, block_len, 2 * width), bf16),
            pltpu.VMEM((ticks + 1, block_len, 2 * width), bf16),
            pltpu.VMEM((block_len, width), bf16),
            pltpu.VMEM((block_len, width), bf16),
            pltpu.VMEM((block_len, hid), bf16),
            pltpu.VMEM((block_len, width), f32),
            pltpu.VMEM((block_len, (NDIL + 1) * block_len), f32),
            pltpu.VMEM((8, LANES), f32),
            pltpu.VMEM((ticks, 8, LANES), f32),
            pltpu.VMEM((ticks, 8, LANES), f32),
            pltpu.VMEM((ticks, 8, LANES), f32),
            pltpu.VMEM((ticks, 8, LANES), f32),
            pltpu.VMEM((ticks, 8, LANES), f32),
            pltpu.VMEM((8, LANES), f32),
            dma((4,)),
            dma,
            dma((ticks,)),
            dma((ticks,)),
            dma((ticks,)),
            dma((ticks,)),
            dma((ticks, PARTS)),
            dma((ticks, PARTS)),
            dma((ticks,)),
            dma((ticks + 1,)),
            dma((ticks,)),
            dma((ticks,)),
            dma((ticks,)),
            dma,
        ],
        compiler_params=pltpu.CompilerParams(
            collective_id=0, has_side_effects=True, vmem_limit_bytes=56 * 1024 * 1024
        ),
        cost_estimate=pl.CostEstimate(
            flops=2 * ticks * block_len * (4 * width * width + 2 * width * hid),
            bytes_accessed=2 * (4 * width * width + 2 * width * hid),
            transcendentals=0,
        ),
    )(
        spins,
        block_mask,
        tok_embed,
        pos_embed,
        norm1_gain,
        w_qkv,
        w_out,
        norm2_gain,
        w_up,
        w_down,
        w_head[None, :],
    )


def solution(mesh):
    return jax.shard_map(
        body,
        mesh=mesh,
        in_specs=(
            P(),
            P("ctx", None),
            P(),
            P("ctx", None),
            P("section", None),
            P("section", None, None),
            P("section", None, None),
            P("section", None),
            P("section", None, None),
            P("section", None, None),
            P(),
        ),
        out_specs=P("section", "ctx"),
        check_vma=False,
    )
```

```python
import functools
import math

import jax
import jax.numpy as jnp
from jax import lax
from jax.experimental import pallas as pl
from jax.experimental.pallas import tpu as pltpu
from jax.sharding import PartitionSpec as P

HEADS = 16
NDIL = 3
CORES = 2
LANES = 128
SOURCES = 2
PARTS = 2
MASKED = -1e30


def rms_normed(vector):
    return vector * lax.rsqrt(jnp.mean(vector * vector, axis=-1, keepdims=True) + 1e-05)


def kernel(
    sections,
    ctx_count,
    spins_ref,
    mask_ref,
    tok_ref,
    pos_hbm,
    gain1_ref,
    wqkv_hbm,
    wout_hbm,
    gain2_ref,
    wup_hbm,
    wdown_hbm,
    whead_ref,
    out_ref,
    wqkv,
    wout,
    wup,
    wdown,
    pos,
    xin,
    xout,
    kv_own,
    kv_far,
    queries,
    attended,
    activated,
    hidden,
    bias,
    mask_send,
    mask_rows,
    totals_send,
    totals_far,
    rows_keep,
    result_send,
    result_in,
    w_sem,
    pos_local_sem,
    pos_send_sem,
    pos_recv_sem,
    mask_send_sem,
    mask_recv_sem,
    x_send_sem,
    x_recv_sem,
    kv_send_sem,
    kv_recv_sem,
    tot_send_sem,
    tot_recv_sem,
    res_send_sem,
    res_recv_sem,
):
    ticks = ctx_count // CORES
    groups = ticks
    block_len, width = pos.shape[1], pos.shape[2]
    part_width = width // PARTS
    hid = wup.shape[1]
    head_dim = width // HEADS
    s = lax.axis_index("section")
    b = lax.axis_index("ctx")
    n = b // CORES
    c = b % CORES
    partner = b + 1 - 2 * c
    last = sections - 1

    def ring(step):
        return lax.rem(n + step, groups)

    w_copies = [
        pltpu.make_async_copy(wqkv_hbm.at[0], wqkv, w_sem.at[0]),
        pltpu.make_async_copy(wout_hbm.at[0], wout, w_sem.at[1]),
        pltpu.make_async_copy(wup_hbm.at[0], wup, w_sem.at[2]),
        pltpu.make_async_copy(wdown_hbm.at[0], wdown, w_sem.at[3]),
    ]
    pos_local = pltpu.make_async_copy(pos_hbm, pos.at[n], pos_local_sem)

    @pl.when(s == 0)
    def _():
        pos_local.start()

    for copy in w_copies:
        copy.start()

    barrier = pltpu.get_barrier_semaphore()

    def greet(section, ctx):
        pl.semaphore_signal(
            barrier, inc=1, device_id=(section, ctx), device_id_type=pl.DeviceIdType.MESH
        )

    greet(s, partner)
    for step in range(1, groups):
        greet(s, ring(step) * CORES + c)

    @pl.when(s == 0)
    def _():
        for source in range(1, SOURCES):
            for step in range(1, groups):
                greet(source, ring(step) * CORES + c)

    @pl.when(s > 0)
    def _():
        greet(s - 1, b)

    result_from = s * CORES + c
    from_self = (s == last) & (b == result_from)

    @pl.when(jnp.logical_not(from_self))
    def _():
        greet(last, result_from)

    lane = lax.broadcasted_iota(jnp.int32, (8, LANES), 1)
    mask_send[...] = jnp.zeros((8, LANES), jnp.float32)
    mask_send[0:1, 0:ctx_count] = mask_ref[...].astype(jnp.float32)
    mask_rows[n] = mask_send[...]

    blank = jnp.zeros((2, block_len, width), jnp.bfloat16)
    for slot in range(1 << (NDIL - 2)):
        kv_own[slot] = blank
    kv_far[0] = blank

    receivers = groups + jnp.where(
        s < last, 1, ticks - jnp.where(n == last, 1, 0)
    ) + jnp.where((s > 0) & (s < SOURCES), groups - 1, 0)
    pl.semaphore_wait(barrier, receivers)

    def remote(src, dst, send_sem, recv_sem, section, ctx):
        return pltpu.make_async_remote_copy(
            src_ref=src,
            dst_ref=dst,
            send_sem=send_sem,
            recv_sem=recv_sem,
            device_id=(section, ctx),
            device_id_type=pl.DeviceIdType.MESH,
        )

    def mask_copy(step):
        return remote(
            mask_send, mask_rows.at[n], mask_send_sem.at[step], mask_recv_sem.at[n],
            s, ring(step) * CORES + c,
        )

    share = block_len // SOURCES

    def pos_copy(step, source):
        rows = pl.ds(source * share, share)
        return remote(
            pos_hbm.at[rows], pos.at[n, rows], pos_send_sem.at[step], pos_recv_sem.at[n, source],
            0, ring(step) * CORES + c,
        )

    for step in range(1, groups):
        mask_copy(step).start()

    for source in range(SOURCES):
        now = (s == source) & (n == 0) if source == 0 else s == source

        @pl.when(now)
        def _():
            for step in range(1, groups):
                pos_copy(step, source).start()

    def mask_arrival(slot):
        return remote(
            mask_send, mask_rows.at[slot], mask_send_sem.at[0], mask_recv_sem.at[slot], s, partner
        )

    def pos_arrival(slot, source):
        rows = pl.ds(source * share, share)
        return remote(
            pos_hbm.at[rows], pos.at[slot, rows], pos_send_sem.at[0], pos_recv_sem.at[slot, source],
            0, partner,
        )

    def x_copy(j, part):
        return remote(
            xout.at[j, part], xin.at[j, part], x_send_sem.at[j, part], x_recv_sem.at[j, part],
            s + 1, b,
        )

    def kv_copy(j, half):
        return remote(
            kv_own.at[j + (1 << (NDIL - 2)), half], kv_far.at[j + 1, half],
            kv_send_sem.at[j, half], kv_recv_sem.at[j + 1, half], s, partner,
        )

    def kv_arrival(slot, half):
        return remote(
            kv_far.at[slot, half], kv_far.at[slot, half], kv_send_sem.at[0, half],
            kv_recv_sem.at[slot, half], s, partner,
        )

    def total_copy(j):
        return remote(
            totals_send.at[j], totals_far.at[j], tot_send_sem.at[j], tot_recv_sem.at[j], s, partner
        )

    row_at = lax.broadcasted_iota(jnp.int32, (block_len, block_len), 0)
    col_at = lax.broadcasted_iota(jnp.int32, (block_len, block_len), 1)

    def spins_row(block):
        at = pl.multiple_of(block * block_len, block_len)
        rows = spins_ref[:, pl.ds(at, block_len)].astype(jnp.float32)
        which = lax.broadcasted_iota(jnp.int32, rows.shape, 0)
        return jnp.sum(jnp.where(which == n, rows, 0.0), axis=0, keepdims=True)

    def tick(j, carry):
        block = j * CORES + c

        @pl.when(j != n)
        def _():
            mask_arrival(j).wait_recv()

        flags = mask_rows[j]
        bias[0:block_len] = jnp.where(row_at <= col_at, 0.0, MASKED).astype(jnp.bfloat16)
        for level in range(NDIL):
            source = block - (1 << level)
            hit = jnp.where((lane == source) & (flags > 0.5), 1.0, 0.0)
            hit = jnp.sum(hit[0:1], axis=1, keepdims=True)
            bias[(level + 1) * block_len : (level + 2) * block_len] = jnp.broadcast_to(
                jnp.where(hit > 0.5, 0.0, MASKED), (block_len, block_len)
            ).astype(jnp.bfloat16)

        @pl.when(s == 0)
        def _():
            @pl.when(j == n)
            def _():
                pos_local.wait()

            @pl.when(j != n)
            def _():
                for source in range(SOURCES):
                    pos_arrival(j, source).wait_recv()

            @pl.when((j == 0) & (n > 0))
            def _():
                for step in range(1, groups):
                    pos_copy(step, 0).start()

            row = spins_row(block)
            before = spins_row(jnp.maximum(block - 1, 0))[:, block_len - 1 : block_len]
            first = jnp.where(block > 0, before, 2.0)
            token = jnp.sum(jnp.where(col_at == row_at - 1, row, 0.0), axis=1, keepdims=True)
            token = jnp.where(row_at[:, 0:1] == 0, first, token)
            rows = jnp.where(
                token == 0.0,
                tok_ref[0:1, :],
                jnp.where(token == 1.0, tok_ref[1:2, :], tok_ref[2:3, :]),
            )
            rows = (rows + pos[j].astype(jnp.float32)).astype(jnp.bfloat16)
            for part in range(PARTS):
                xin[j, part] = rows[:, part * part_width : (part + 1) * part_width]

        @pl.when(s > 0)
        def _():
            for part in range(PARTS):
                remote(
                    xout.at[j, part], xin.at[j, part], x_send_sem.at[j, part],
                    x_recv_sem.at[j, part], s, partner,
                ).wait_recv()

        layer_in = jnp.concatenate([xin[j, part] for part in range(PARTS)], axis=1)
        layer_in = layer_in.astype(jnp.float32)
        hidden[...] = layer_in
        normed = (rms_normed(layer_in) * gain1_ref[...]).astype(jnp.bfloat16)

        @pl.when(j == 0)
        def _():
            w_copies[0].wait()

        own = j + (1 << (NDIL - 2))
        for half in range(2):
            for chunk in range(0, width, 512):
                at = (half + 1) * width + chunk
                kv_own[own, half, :, chunk : chunk + 512] = jnp.dot(
                    normed, wqkv[:, at : at + 512], preferred_element_type=jnp.float32
                ).astype(jnp.bfloat16)

            @pl.when((c == 0) | (j < ticks - 1))
            def _():
                kv_copy(j, half).start()

        for chunk in range(0, width, 512):
            queries[:, chunk : chunk + 512] = (
                jnp.dot(normed, wqkv[:, chunk : chunk + 512], preferred_element_type=jnp.float32)
                * (math.log2(math.e) / math.sqrt(head_dim))
            ).astype(jnp.bfloat16)

        @pl.when(j + c > 0)
        def _():
            for half in range(2):
                kv_arrival(j + c, half).wait_recv()

        lane_low = lax.broadcasted_iota(jnp.int32, (block_len, LANES), 1) < head_dim
        one_hot = jnp.where(row_at == col_at, 1.0, 0.0).astype(jnp.bfloat16)
        one_hot = jnp.concatenate([one_hot, one_hot], axis=0)

        def attend(slots):
            pairs = width // LANES
            biases = bias[0 : len(slots) * block_len]
            ones = jnp.ones((len(slots) * block_len, LANES), jnp.bfloat16)

            def scores_of(pair):
                cols = slice(pair * LANES, (pair + 1) * LANES)
                q_pair = queries[:, cols]
                zero = jnp.zeros_like(q_pair)
                q_two = jnp.concatenate(
                    [jnp.where(lane_low, q_pair, zero), jnp.where(lane_low, zero, q_pair)], axis=0
                )
                keys = jnp.concatenate([ref[at, 0, :, cols] for ref, at in slots], axis=0)
                return lax.dot_general(
                    jnp.concatenate([q_two, one_hot], axis=1),
                    jnp.concatenate([keys, biases], axis=1),
                    (((1,), (1,)), ((), ())),
                    preferred_element_type=jnp.float32,
                )

            pending = scores_of(0)
            for pair in range(pairs):
                cols = slice(pair * LANES, (pair + 1) * LANES)
                scores = pending
                if pair + 1 < pairs:
                    pending = scores_of(pair + 1)
                top = jnp.max(scores, axis=1, keepdims=True)
                probs = jnp.exp2(scores - top).astype(jnp.bfloat16)
                values = jnp.concatenate([ref[at, 1, :, cols] for ref, at in slots], axis=0)
                mixed = jnp.dot(
                    probs,
                    jnp.concatenate([values, ones], axis=1),
                    preferred_element_type=jnp.float32,
                )
                mixed = jnp.where(
                    jnp.concatenate([lane_low, lane_low], axis=1),
                    mixed[:block_len],
                    mixed[block_len:],
                )
                attended[:, cols] = (mixed[:, :LANES] / mixed[:, LANES:]).astype(jnp.bfloat16)

        key_slots = [(kv_own, own), (kv_far, j + c)]
        for level in range(1, NDIL):
            key_slots.append((kv_own, own - (1 << (level - 1))))

        @pl.when(j == 0)
        def _():
            attend(key_slots[:2])

        @pl.when(j > 0)
        def _():
            attend(key_slots)

        @pl.when(j == 0)
        def _():
            w_copies[1].wait()

        att = attended[...]
        for chunk in range(0, width, 512):
            hidden[:, chunk : chunk + 512] += jnp.dot(
                att, wout[:, chunk : chunk + 512], preferred_element_type=jnp.float32
            )
        lifted = (rms_normed(hidden[...]) * gain2_ref[...]).astype(jnp.bfloat16)

        @pl.when(j == 0)
        def _():
            w_copies[2].wait()

        for chunk in range(0, hid, 512):
            activated[:, chunk : chunk + 512] = jax.nn.gelu(
                jnp.dot(lifted, wup[:, chunk : chunk + 512], preferred_element_type=jnp.float32)
            ).astype(jnp.bfloat16)

        @pl.when(j == 0)
        def _():
            w_copies[3].wait()

        act = activated[...]
        for part in range(PARTS):
            cols = slice(part * part_width, (part + 1) * part_width)
            xout[j, part] = (
                hidden[:, cols]
                + jnp.dot(act, wdown[:, cols], preferred_element_type=jnp.float32)
            ).astype(jnp.bfloat16)

            @pl.when(s < last)
            def _():
                x_copy(j, part).start()

        @pl.when(s == last)
        def _():
            final = jnp.concatenate([xout[j, part] for part in range(PARTS)], axis=1)
            final = rms_normed(final.astype(jnp.float32))
            logits = jnp.sum(final * whead_ref[...], axis=1, keepdims=True)
            spin_col = jnp.sum(
                jnp.where(col_at == row_at, spins_row(block), 0.0), axis=1, keepdims=True
            )
            signed = (1.0 - 2.0 * spin_col) * logits
            soft = jnp.maximum(signed, 0.0) + jnp.log1p(jnp.exp(-jnp.abs(signed)))
            terms = math.log(2.0) - soft
            running = jnp.sum(jnp.where(row_at <= col_at, terms, 0.0), axis=0, keepdims=True)
            total = jnp.sum(terms, axis=0, keepdims=True)
            rows_keep[j] = jnp.broadcast_to(running, (8, LANES))
            totals_send[j] = jnp.broadcast_to(total, (8, LANES))
            total_copy(j).start()

        return carry

    lax.fori_loop(0, ticks, tick, 0)

    def result_copy(j, section, ctx):
        return remote(
            result_send.at[j], result_in, res_send_sem.at[j], res_recv_sem, section, ctx
        )

    @pl.when(s == last)
    def _():
        offset = jnp.zeros((8, LANES), jnp.float32)
        for j in range(ticks):
            total_copy(j).wait_recv()
            own_total = totals_send[j]
            far_total = totals_far[j]
            before = offset + far_total * c.astype(jnp.float32)
            result = 0.5 * (rows_keep[j] + before)
            result_send[j] = result
            offset = offset + (own_total + far_total)
            to_self = (n == last) & (j == last)

            @pl.when(to_self)
            def _():
                result_in[...] = result

            @pl.when(jnp.logical_not(to_self))
            def _():
                result_copy(j, n, j * CORES + c).start()

    @pl.when(jnp.logical_not(from_self))
    def _():
        result_copy(0, s, partner).wait_recv()

    out_ref[...] = result_in[0:1, :]

    for step in range(1, groups):
        mask_copy(step).wait_send()

    for source in range(SOURCES):
        @pl.when(s == source)
        def _():
            for step in range(1, groups):
                pos_copy(step, source).wait_send()

    for j in range(ticks):
        @pl.when((c == 0) | (j < ticks - 1))
        def _():
            for half in range(2):
                kv_copy(j, half).wait_send()

        @pl.when(s < last)
        def _():
            for part in range(PARTS):
                x_copy(j, part).wait_send()

        @pl.when(s == last)
        def _():
            total_copy(j).wait_send()

            @pl.when(jnp.logical_not((n == last) & (j == last)))
            def _():
                result_copy(j, n, j * CORES + c).wait_send()


def body(
    spins,
    block_mask,
    tok_embed,
    pos_embed,
    norm1_gain,
    w_qkv,
    w_out,
    norm2_gain,
    w_up,
    w_down,
    w_head,
):
    sections = lax.axis_size("section")
    ctx_count = lax.axis_size("ctx")
    ticks = ctx_count // CORES
    block_len, width = pos_embed.shape
    hid = w_up.shape[2]
    assert ticks == sections == spins.shape[0] and block_len == LANES
    bf16, f32 = jnp.bfloat16, jnp.float32
    vmem = pl.BlockSpec(memory_space=pltpu.VMEM)
    hbm = pl.BlockSpec(memory_space=pltpu.HBM)
    back = 1 << (NDIL - 2)
    dma = pltpu.SemaphoreType.DMA
    return pl.pallas_call(
        functools.partial(kernel, sections, ctx_count),
        out_shape=jax.ShapeDtypeStruct((1, block_len), f32),
        in_specs=[vmem, vmem, vmem, hbm, vmem, hbm, hbm, vmem, hbm, hbm, vmem],
        out_specs=vmem,
        scratch_shapes=[
            pltpu.VMEM((width, 3 * width), bf16),
            pltpu.VMEM((width, width), bf16),
            pltpu.VMEM((width, hid), bf16),
            pltpu.VMEM((hid, width), bf16),
            pltpu.VMEM((ticks, block_len, width), bf16),
            pltpu.VMEM((ticks, PARTS, block_len, width // PARTS), bf16),
            pltpu.VMEM((ticks, PARTS, block_len, width // PARTS), bf16),
            pltpu.VMEM((ticks + back, 2, block_len, width), bf16),
            pltpu.VMEM((ticks + 1, 2, block_len, width), bf16),
            pltpu.VMEM((block_len, width), bf16),
            pltpu.VMEM((block_len, width), bf16),
            pltpu.VMEM((block_len, hid), bf16),
            pltpu.VMEM((block_len, width), f32),
            pltpu.VMEM(((NDIL + 1) * block_len, block_len), bf16),
            pltpu.VMEM((8, LANES), f32),
            pltpu.VMEM((ticks, 8, LANES), f32),
            pltpu.VMEM((ticks, 8, LANES), f32),
            pltpu.VMEM((ticks, 8, LANES), f32),
            pltpu.VMEM((ticks, 8, LANES), f32),
            pltpu.VMEM((ticks, 8, LANES), f32),
            pltpu.VMEM((8, LANES), f32),
            dma((4,)),
            dma,
            dma((ticks,)),
            dma((ticks, SOURCES)),
            dma((ticks,)),
            dma((ticks,)),
            dma((ticks, PARTS)),
            dma((ticks, PARTS)),
            dma((ticks, 2)),
            dma((ticks + 1, 2)),
            dma((ticks,)),
            dma((ticks,)),
            dma((ticks,)),
            dma,
        ],
        compiler_params=pltpu.CompilerParams(
            collective_id=0, has_side_effects=True, vmem_limit_bytes=56 * 1024 * 1024
        ),
        cost_estimate=pl.CostEstimate(
            flops=2 * ticks * block_len * (4 * width * width + 2 * width * hid),
            bytes_accessed=2 * (4 * width * width + 2 * width * hid),
            transcendentals=0,
        ),
    )(
        spins,
        block_mask,
        tok_embed,
        pos_embed,
        norm1_gain,
        w_qkv,
        w_out,
        norm2_gain,
        w_up,
        w_down,
        w_head[None, :],
    )


def solution(mesh):
    return jax.shard_map(
        body,
        mesh=mesh,
        in_specs=(
            P(),
            P("ctx", None),
            P(),
            P("ctx", None),
            P("section", None),
            P("section", None, None),
            P("section", None, None),
            P("section", None),
            P("section", None, None),
            P("section", None, None),
            P(),
        ),
        out_specs=P("section", "ctx"),
        check_vma=False,
    )
```

```python
import functools
import math

import jax
import jax.numpy as jnp
from jax import lax
from jax.experimental import pallas as pl
from jax.experimental.pallas import tpu as pltpu
from jax.sharding import PartitionSpec as P

HEADS = 16
NDIL = 3
COLS = 1024
CORES = 2
LANES = 128
SOURCES = 2
PARTS = 2
MASKED = -1e30


def rms_normed(vector):
    return vector * lax.rsqrt(jnp.mean(vector * vector, axis=-1, keepdims=True) + 1e-05)


def kernel(
    sections,
    ctx_count,
    spins_ref,
    mask_ref,
    tok_ref,
    pos_hbm,
    gain1_ref,
    wqkv_hbm,
    wout_hbm,
    gain2_ref,
    wup_hbm,
    wdown_hbm,
    whead_ref,
    out_ref,
    wqkv,
    wout,
    wup,
    wdown,
    pos,
    xin,
    xout,
    kv_own,
    kv_far,
    queries,
    attended,
    activated,
    hidden,
    bias,
    mask_send,
    mask_rows,
    totals_send,
    totals_far,
    rows_keep,
    result_send,
    result_in,
    w_sem,
    pos_local_sem,
    pos_send_sem,
    pos_recv_sem,
    mask_send_sem,
    mask_recv_sem,
    x_send_sem,
    x_recv_sem,
    kv_send_sem,
    kv_recv_sem,
    tot_send_sem,
    tot_recv_sem,
    res_send_sem,
    res_recv_sem,
    turn_sem,
    offset,
):
    ticks = ctx_count // CORES
    groups = ticks
    block_len, width = pos.shape[1], pos.shape[2]
    part_width = width // PARTS
    hid = wup.shape[1]
    head_dim = width // HEADS
    s = lax.axis_index("section")
    b = lax.axis_index("ctx")
    n = b // CORES
    c = b % CORES
    partner = b + 1 - 2 * c
    last = sections - 1

    def ring(step):
        return lax.rem(n + step, groups)

    w_copies = [
        pltpu.make_async_copy(wqkv_hbm.at[0], wqkv, w_sem.at[0]),
        pltpu.make_async_copy(wout_hbm.at[0], wout, w_sem.at[1]),
        pltpu.make_async_copy(wup_hbm.at[0], wup, w_sem.at[2]),
        pltpu.make_async_copy(wdown_hbm.at[0], wdown, w_sem.at[3]),
    ]
    pos_local = pltpu.make_async_copy(pos_hbm, pos.at[n], pos_local_sem)

    @pl.when(s == 0)
    def _():
        pos_local.start()

    for copy in w_copies:
        copy.start()

    barrier = pltpu.get_barrier_semaphore()

    def greet(section, ctx):
        pl.semaphore_signal(
            barrier, inc=1, device_id=(section, ctx), device_id_type=pl.DeviceIdType.MESH
        )

    greet(s, partner)
    for step in range(1, groups):
        greet(s, ring(step) * CORES + c)

    @pl.when(s == 0)
    def _():
        for source in range(1, SOURCES):
            for step in range(1, groups):
                greet(source, ring(step) * CORES + c)

    @pl.when(s > 0)
    def _():
        greet(s - 1, b)

    result_from = s * CORES + c
    from_self = (s == last) & (b == result_from)

    @pl.when(jnp.logical_not(from_self))
    def _():
        greet(last, result_from)

    lane = lax.broadcasted_iota(jnp.int32, (8, LANES), 1)
    mask_send[...] = jnp.zeros((8, LANES), jnp.float32)
    mask_send[0:1, 0:ctx_count] = mask_ref[...].astype(jnp.float32)
    mask_rows[n] = mask_send[...]

    blank = jnp.zeros((2, block_len, width), jnp.bfloat16)
    for slot in range(1 << (NDIL - 2)):
        kv_own[slot] = blank
    kv_far[0] = blank

    receivers = groups + jnp.where(
        s < last, 1, ticks - jnp.where(n == last, 1, 0)
    ) + jnp.where((s > 0) & (s < SOURCES), groups - 1, 0)
    pl.semaphore_wait(barrier, receivers)

    def remote(src, dst, send_sem, recv_sem, section, ctx):
        return pltpu.make_async_remote_copy(
            src_ref=src,
            dst_ref=dst,
            send_sem=send_sem,
            recv_sem=recv_sem,
            device_id=(section, ctx),
            device_id_type=pl.DeviceIdType.MESH,
        )

    def mask_copy(step):
        return remote(
            mask_send, mask_rows.at[n], mask_send_sem.at[step], mask_recv_sem.at[n],
            s, ring(step) * CORES + c,
        )

    share = block_len // SOURCES

    def pos_copy(step, source):
        rows = pl.ds(source * share, share)
        return remote(
            pos_hbm.at[rows], pos.at[n, rows], pos_send_sem.at[step], pos_recv_sem.at[n, source],
            0, ring(step) * CORES + c,
        )

    for step in range(1, groups):
        mask_copy(step).start()

    for source in range(SOURCES):
        @pl.when((s == source) & (n == 0) & (c == 1))
        def _():
            pl.semaphore_wait(turn_sem, 1)

        now = (s == source) & (n == 0) if source == 0 else s == source

        @pl.when(now)
        def _():
            for step in range(1, groups):
                pos_copy(step, source).start()

        @pl.when((s == source) & (n == 0) & (c == 0))
        def _():
            for step in range(1, groups):
                pos_copy(step, source).wait_send()
            pl.semaphore_signal(
                turn_sem, inc=1, device_id=(s, partner), device_id_type=pl.DeviceIdType.MESH
            )

    def mask_arrival(slot):
        return remote(
            mask_send, mask_rows.at[slot], mask_send_sem.at[0], mask_recv_sem.at[slot], s, partner
        )

    def pos_arrival(slot, source):
        rows = pl.ds(source * share, share)
        return remote(
            pos_hbm.at[rows], pos.at[slot, rows], pos_send_sem.at[0], pos_recv_sem.at[slot, source],
            0, partner,
        )

    def x_copy(j, part):
        return remote(
            xout.at[j, part], xin.at[j, part], x_send_sem.at[j, part], x_recv_sem.at[j, part],
            s + 1, b,
        )

    def kv_copy(j, half):
        return remote(
            kv_own.at[j + (1 << (NDIL - 2)), half], kv_far.at[j + 1, half],
            kv_send_sem.at[j, half], kv_recv_sem.at[j + 1, half], s, partner,
        )

    def kv_arrival(slot, half):
        return remote(
            kv_far.at[slot, half], kv_far.at[slot, half], kv_send_sem.at[0, half],
            kv_recv_sem.at[slot, half], s, partner,
        )

    def total_copy(j):
        return remote(
            totals_send.at[j], totals_far.at[j], tot_send_sem.at[j], tot_recv_sem.at[j], s, partner
        )

    row_at = lax.broadcasted_iota(jnp.int32, (block_len, block_len), 0)
    col_at = lax.broadcasted_iota(jnp.int32, (block_len, block_len), 1)

    def spins_row(block):
        at = pl.multiple_of(block * block_len, block_len)
        rows = spins_ref[:, pl.ds(at, block_len)].astype(jnp.float32)
        which = lax.broadcasted_iota(jnp.int32, rows.shape, 0)
        return jnp.sum(jnp.where(which == n, rows, 0.0), axis=0, keepdims=True)

    def tick(j, carry):
        block = j * CORES + c

        @pl.when(s == 0)
        def _():
            @pl.when(j == n)
            def _():
                pos_local.wait()

            @pl.when(j != n)
            def _():
                for source in range(SOURCES):
                    pos_arrival(j, source).wait_recv()

            @pl.when((j == 0) & (n > 0))
            def _():
                for step in range(1, groups):
                    pos_copy(step, 0).start()

            row = spins_row(block)
            before = spins_row(jnp.maximum(block - 1, 0))[:, block_len - 1 : block_len]
            first = jnp.where(block > 0, before, 2.0)
            token = jnp.sum(jnp.where(col_at == row_at - 1, row, 0.0), axis=1, keepdims=True)
            token = jnp.where(row_at[:, 0:1] == 0, first, token)
            rows = jnp.where(
                token == 0.0,
                tok_ref[0:1, :],
                jnp.where(token == 1.0, tok_ref[1:2, :], tok_ref[2:3, :]),
            )
            rows = (rows + pos[j].astype(jnp.float32)).astype(jnp.bfloat16)
            for part in range(PARTS):
                xin[j, part] = rows[:, part * part_width : (part + 1) * part_width]

        @pl.when(s > 0)
        def _():
            for part in range(PARTS):
                remote(
                    xout.at[j, part], xin.at[j, part], x_send_sem.at[j, part],
                    x_recv_sem.at[j, part], s, partner,
                ).wait_recv()

        layer_in = jnp.concatenate([xin[j, part] for part in range(PARTS)], axis=1)
        layer_in = layer_in.astype(jnp.float32)
        hidden[...] = layer_in
        normed = (rms_normed(layer_in) * gain1_ref[...]).astype(jnp.bfloat16)

        flags = mask_rows[j]
        bias[0:block_len] = jnp.where(row_at <= col_at, 0.0, MASKED).astype(jnp.bfloat16)
        for level in range(NDIL):
            source = block - (1 << level)
            hit = jnp.where((lane == source) & (flags > 0.5), 1.0, 0.0)
            hit = jnp.sum(hit[0:1], axis=1, keepdims=True)
            bias[(level + 1) * block_len : (level + 2) * block_len] = jnp.broadcast_to(
                jnp.where(hit > 0.5, 0.0, MASKED), (block_len, block_len)
            ).astype(jnp.bfloat16)

        own = j + (1 << (NDIL - 2))
        for half in range(2):
            for chunk in range(0, width, COLS):
                at = (half + 1) * width + chunk
                kv_own[own, half, :, chunk : chunk + COLS] = jnp.dot(
                    normed, wqkv[:, at : at + COLS], preferred_element_type=jnp.float32
                ).astype(jnp.bfloat16)

            kv_copy(j, half).start()

        for chunk in range(0, width, COLS):
            queries[:, chunk : chunk + COLS] = (
                jnp.dot(normed, wqkv[:, chunk : chunk + COLS], preferred_element_type=jnp.float32)
                * (math.log2(math.e) / math.sqrt(head_dim))
            ).astype(jnp.bfloat16)

        @pl.when(j + c > 0)
        def _():
            for half in range(2):
                kv_arrival(j + c, half).wait_recv()

        lane_low = lax.broadcasted_iota(jnp.int32, (block_len, LANES), 1) < head_dim
        one_hot = jnp.where(row_at == col_at, 1.0, 0.0).astype(jnp.bfloat16)
        one_hot = jnp.concatenate([one_hot, one_hot], axis=0)

        def attend(slots):
            pairs = width // LANES
            biases = bias[0 : len(slots) * block_len]
            ones = jnp.ones((len(slots) * block_len, LANES), jnp.bfloat16)

            def scores_of(pair):
                cols = slice(pair * LANES, (pair + 1) * LANES)
                q_pair = queries[:, cols]
                zero = jnp.zeros_like(q_pair)
                q_two = jnp.concatenate(
                    [jnp.where(lane_low, q_pair, zero), jnp.where(lane_low, zero, q_pair)], axis=0
                )
                keys = jnp.concatenate([ref[at, 0, :, cols] for ref, at in slots], axis=0)
                return lax.dot_general(
                    jnp.concatenate([q_two, one_hot], axis=1),
                    jnp.concatenate([keys, biases], axis=1),
                    (((1,), (1,)), ((), ())),
                    preferred_element_type=jnp.float32,
                )

            pending = scores_of(0)
            for pair in range(pairs):
                cols = slice(pair * LANES, (pair + 1) * LANES)
                scores = pending
                if pair + 1 < pairs:
                    pending = scores_of(pair + 1)
                top = jnp.max(scores, axis=1, keepdims=True)
                probs = jnp.exp2(scores - top).astype(jnp.bfloat16)
                values = jnp.concatenate([ref[at, 1, :, cols] for ref, at in slots], axis=0)
                mixed = jnp.dot(
                    probs,
                    jnp.concatenate([values, ones], axis=1),
                    preferred_element_type=jnp.float32,
                )
                mixed = jnp.where(
                    jnp.concatenate([lane_low, lane_low], axis=1),
                    mixed[:block_len],
                    mixed[block_len:],
                )
                attended[:, cols] = (mixed[:, :LANES] / mixed[:, LANES:]).astype(jnp.bfloat16)

        key_slots = [(kv_own, own), (kv_far, j + c)]
        for level in range(1, NDIL):
            key_slots.append((kv_own, own - (1 << (level - 1))))

        @pl.when(j == 0)
        def _():
            attend(key_slots[:2])

        @pl.when(j > 0)
        def _():
            attend(key_slots)

        att = attended[...]
        for chunk in range(0, width, COLS):
            hidden[:, chunk : chunk + COLS] += jnp.dot(
                att, wout[:, chunk : chunk + COLS], preferred_element_type=jnp.float32
            )
        lifted = (rms_normed(hidden[...]) * gain2_ref[...]).astype(jnp.bfloat16)

        for chunk in range(0, hid, COLS):
            activated[:, chunk : chunk + COLS] = jax.nn.gelu(
                jnp.dot(lifted, wup[:, chunk : chunk + COLS], preferred_element_type=jnp.float32)
            ).astype(jnp.bfloat16)

        act = activated[...]
        for part in range(PARTS):
            cols = slice(part * part_width, (part + 1) * part_width)
            xout[j, part] = (
                hidden[:, cols]
                + jnp.dot(act, wdown[:, cols], preferred_element_type=jnp.float32)
            ).astype(jnp.bfloat16)

            @pl.when(s < last)
            def _():
                x_copy(j, part).start()

        @pl.when(s == last)
        def _():
            final = jnp.concatenate([xout[j, part] for part in range(PARTS)], axis=1)
            final = rms_normed(final.astype(jnp.float32))
            logits = jnp.sum(final * whead_ref[...], axis=1, keepdims=True)
            spin_col = jnp.sum(
                jnp.where(col_at == row_at, spins_row(block), 0.0), axis=1, keepdims=True
            )
            signed = (1.0 - 2.0 * spin_col) * logits
            soft = jnp.maximum(signed, 0.0) + jnp.log1p(jnp.exp(-jnp.abs(signed)))
            terms = math.log(2.0) - soft
            running = jnp.sum(jnp.where(row_at <= col_at, terms, 0.0), axis=0, keepdims=True)
            total = jnp.sum(terms, axis=0, keepdims=True)
            rows_keep[j] = jnp.broadcast_to(running, (8, LANES))
            totals_send[j] = jnp.broadcast_to(total, (8, LANES))
            total_copy(j).start()

        return carry

    for step in range(1, groups):
        mask_arrival(ring(step)).wait_recv()
    for copy in w_copies:
        copy.wait()

    lax.fori_loop(0, ticks, tick, 0)

    def result_copy(j, section, ctx):
        return remote(
            result_send.at[j], result_in, res_send_sem.at[j], res_recv_sem, section, ctx
        )

    @pl.when(s == last)
    def _():
        offset[...] = jnp.zeros((8, LANES), jnp.float32)
        for j in range(ticks):
            @pl.when(c == 0)
            def _():
                result_send[j] = 0.5 * (rows_keep[j] + offset[...])

            @pl.when(c == 1)
            def _():
                total_copy(j).wait_recv()
                result_send[j] = 0.5 * (rows_keep[j] + (offset[...] + totals_far[j]))

            to_self = (n == last) & (j == last)

            @pl.when(to_self)
            def _():
                result_in[...] = result_send[j]

            @pl.when(jnp.logical_not(to_self))
            def _():
                result_copy(j, n, j * CORES + c).start()

            @pl.when(c == 0)
            def _():
                total_copy(j).wait_recv()

            offset[...] += totals_send[j] + totals_far[j]

    @pl.when(jnp.logical_not(from_self))
    def _():
        result_copy(0, s, partner).wait_recv()

    out_ref[...] = result_in[0:1, :]

    @pl.when(c == 0)
    def _():
        for half in range(2):
            kv_arrival(ticks, half).wait_recv()

    for step in range(1, groups):
        mask_copy(step).wait_send()

    for source in range(SOURCES):
        @pl.when((s == source) & (b > 0))
        def _():
            for step in range(1, groups):
                pos_copy(step, source).wait_send()

    for j in range(ticks):
        for half in range(2):
            kv_copy(j, half).wait_send()

        @pl.when(s < last)
        def _():
            for part in range(PARTS):
                x_copy(j, part).wait_send()

        @pl.when(s == last)
        def _():
            total_copy(j).wait_send()

            @pl.when(jnp.logical_not((n == last) & (j == last)))
            def _():
                result_copy(j, n, j * CORES + c).wait_send()


def body(
    spins,
    block_mask,
    tok_embed,
    pos_embed,
    norm1_gain,
    w_qkv,
    w_out,
    norm2_gain,
    w_up,
    w_down,
    w_head,
):
    sections = lax.axis_size("section")
    ctx_count = lax.axis_size("ctx")
    ticks = ctx_count // CORES
    block_len, width = pos_embed.shape
    hid = w_up.shape[2]
    assert ticks == sections == spins.shape[0] and block_len == LANES
    bf16, f32 = jnp.bfloat16, jnp.float32
    vmem = pl.BlockSpec(memory_space=pltpu.VMEM)
    hbm = pl.BlockSpec(memory_space=pltpu.HBM)
    back = 1 << (NDIL - 2)
    dma = pltpu.SemaphoreType.DMA
    return pl.pallas_call(
        functools.partial(kernel, sections, ctx_count),
        out_shape=jax.ShapeDtypeStruct((1, block_len), f32),
        in_specs=[vmem, vmem, vmem, hbm, vmem, hbm, hbm, vmem, hbm, hbm, vmem],
        out_specs=vmem,
        scratch_shapes=[
            pltpu.VMEM((width, 3 * width), bf16),
            pltpu.VMEM((width, width), bf16),
            pltpu.VMEM((width, hid), bf16),
            pltpu.VMEM((hid, width), bf16),
            pltpu.VMEM((ticks, block_len, width), bf16),
            pltpu.VMEM((ticks, PARTS, block_len, width // PARTS), bf16),
            pltpu.VMEM((ticks, PARTS, block_len, width // PARTS), bf16),
            pltpu.VMEM((ticks + back, 2, block_len, width), bf16),
            pltpu.VMEM((ticks + 1, 2, block_len, width), bf16),
            pltpu.VMEM((block_len, width), bf16),
            pltpu.VMEM((block_len, width), bf16),
            pltpu.VMEM((block_len, hid), bf16),
            pltpu.VMEM((block_len, width), f32),
            pltpu.VMEM(((NDIL + 1) * block_len, block_len), bf16),
            pltpu.VMEM((8, LANES), f32),
            pltpu.VMEM((ticks, 8, LANES), f32),
            pltpu.VMEM((ticks, 8, LANES), f32),
            pltpu.VMEM((ticks, 8, LANES), f32),
            pltpu.VMEM((ticks, 8, LANES), f32),
            pltpu.VMEM((ticks, 8, LANES), f32),
            pltpu.VMEM((8, LANES), f32),
            dma((4,)),
            dma,
            dma((ticks,)),
            dma((ticks, SOURCES)),
            dma((ticks,)),
            dma((ticks,)),
            dma((ticks, PARTS)),
            dma((ticks, PARTS)),
            dma((ticks, 2)),
            dma((ticks + 1, 2)),
            dma((ticks,)),
            dma((ticks,)),
            dma((ticks,)),
            dma,
            pltpu.SemaphoreType.REGULAR,
            pltpu.VMEM((8, LANES), f32),
        ],
        compiler_params=pltpu.CompilerParams(
            collective_id=0, has_side_effects=True, vmem_limit_bytes=56 * 1024 * 1024
        ),
        cost_estimate=pl.CostEstimate(
            flops=2 * ticks * block_len * (4 * width * width + 2 * width * hid),
            bytes_accessed=2 * (4 * width * width + 2 * width * hid),
            transcendentals=0,
        ),
    )(
        spins,
        block_mask,
        tok_embed,
        pos_embed,
        norm1_gain,
        w_qkv,
        w_out,
        norm2_gain,
        w_up,
        w_down,
        w_head[None, :],
    )


def solution(mesh):
    return jax.shard_map(
        body,
        mesh=mesh,
        in_specs=(
            P(),
            P("ctx", None),
            P(),
            P("ctx", None),
            P("section", None),
            P("section", None, None),
            P("section", None, None),
            P("section", None),
            P("section", None, None),
            P("section", None, None),
            P(),
        ),
        out_specs=P("section", "ctx"),
        check_vma=False,
    )
```
